32 devices in a mesh: row: 4 (over z), col: 8 (over y, x, core).
Axes of the slice: x: 2, y: 2, z: 4, core: 2. Of those that a mesh axis runs over, the one named last changes fastest.
Arguments:
- inputs: bfloat16 [256, 8192], P('col', 'row'), may hold values from -6 to 6
- out_grad: bfloat16 [256, 8192], P('col', 'row'), may hold values from -6 to 6
- w_gate: bfloat16 [8192, 16384], P('row', 'col'), may hold values from -0.0625 to 0.0625
- w_up: bfloat16 [8192, 16384], P('row', 'col'), may hold values from -0.0625 to 0.0625
- w_down: bfloat16 [16384, 8192], P('col', 'row'), may hold values from -0.046875 to 0.046875
Outputs:
- input_grad: bfloat16 [256, 8192], P('col', 'row')
- gate_wgrad: bfloat16 [8192, 16384], P('row', 'col')
- up_wgrad: bfloat16 [8192, 16384], P('row', 'col')
- down_wgrad: bfloat16 [16384, 8192], P('col', 'row')
The draws below stay inside these ranges and needn't reach their ends.
All inputs are finite; a program needn't handle non-finite values.
Results may differ from the reference program's by a relative error of at most 0.02.
Values may be sent and summed in bfloat16 or wider, within the bound.
A program may use at most 128 MiB of HBM per device.

```python
import jax
import jax.numpy as jnp
from jax import lax

D = 8192
F = 16384
TOKENS = 256
N_ROW = 4
N_COL = 8


def block_scale(own_key, dims, pieces, low, top_value):
    def one(dim, parts):
        steps = jax.random.uniform(jax.random.fold_in(jax.random.fold_in(own_key, 6), dim), (parts,), jnp.float32, low / len(pieces), top_value / len(pieces))
        return jnp.repeat(jnp.exp(steps), dims[dim] // parts).reshape((-1,) + (1,) * (len(dims) - dim - 1))

    loudness = one(*pieces[0])
    for cut in pieces[1:]:
        loudness = loudness * one(*cut)
    return loudness


def bell_draw(stream_key, dims, scale, most, cuts=(), kind=jnp.bfloat16):
    loudness = block_scale(stream_key, dims, cuts, -0.22, 0.18) if cuts else 1.0
    drawn = jax.random.normal(stream_key, dims, jnp.float32) * scale * loudness
    return jnp.minimum(jnp.maximum(drawn, -most), most).astype(kind)


def setup_inputs(seed: int = 0) -> dict:
    seeds = jax.random.split(jax.random.key(seed), 6)
    inputs = bell_draw(seeds[0], (TOKENS, D), 1.0, 6.0, ((0, 8), (1, 4)))
    out_grad = bell_draw(seeds[1], (TOKENS, D), 1.0, 6.0, ((0, 8), (1, 4)))
    w_gate = bell_draw(seeds[2], (D, F), D ** -0.5, 0.0625, ((0, 4), (1, 8)))
    w_up = bell_draw(seeds[3], (D, F), D ** -0.5, 0.0625, ((0, 4), (1, 8)))
    w_down = bell_draw(seeds[4], (F, D), F ** -0.5, 0.046875, ((0, 8), (1, 4)))
    return dict(inputs=inputs, out_grad=out_grad, w_gate=w_gate, w_up=w_up, w_down=w_down)


def rounded(term):
    return lax.optimization_barrier(term.astype(jnp.bfloat16)).astype(jnp.float32)


def reference(inputs, out_grad, w_gate, w_up, w_down):
    tokens = inputs.shape[0]
    feat_block = D // N_ROW
    hid_block = F // N_COL
    rest = (((1,), (1,)), ((), ()))

    def feature_step(carry, index):
        start = (index * feat_block).astype(jnp.int32)
        in_block = lax.dynamic_slice_in_dim(inputs, start, feat_block, 1)
        co_block = lax.dynamic_slice_in_dim(out_grad, start, feat_block, 1)
        wg_block = lax.dynamic_slice_in_dim(w_gate, start, feat_block, 0)
        wu_block = lax.dynamic_slice_in_dim(w_up, start, feat_block, 0)
        wd_block = lax.dynamic_slice_in_dim(w_down, start, feat_block, 1)
        gate_acc, up_acc, back_acc = carry
        gate_acc = gate_acc + rounded(jnp.dot(in_block, wg_block, preferred_element_type=jnp.float32))
        up_acc = up_acc + rounded(jnp.dot(in_block, wu_block, preferred_element_type=jnp.float32))
        back_acc = back_acc + rounded(lax.dot_general(co_block, wd_block, rest, preferred_element_type=jnp.float32))
        return (gate_acc, up_acc, back_acc), None

    zeros_hidden = jnp.zeros((tokens, F), jnp.float32)
    (gate, up, hidden_grad), _ = lax.scan(feature_step, (zeros_hidden, zeros_hidden, zeros_hidden), jnp.arange(N_ROW, dtype=jnp.int32))
    sig = jax.nn.sigmoid(gate)
    act = gate * sig
    hidden = (act * up).astype(jnp.bfloat16)
    up_delta = (hidden_grad * act).astype(jnp.bfloat16)
    gate_delta = (hidden_grad * up * sig * (1.0 + gate * (1.0 - sig))).astype(jnp.bfloat16)

    def hidden_step(carry, index):
        start = (index * hid_block).astype(jnp.int32)
        gd_block = lax.dynamic_slice_in_dim(gate_delta, start, hid_block, 1)
        ud_block = lax.dynamic_slice_in_dim(up_delta, start, hid_block, 1)
        wg_block = lax.dynamic_slice_in_dim(w_gate, start, hid_block, 1)
        wu_block = lax.dynamic_slice_in_dim(w_up, start, hid_block, 1)
        first = lax.dot_general(gd_block, wg_block, rest, preferred_element_type=jnp.float32)
        second = lax.dot_general(ud_block, wu_block, rest, preferred_element_type=jnp.float32)
        return carry + rounded(first + second), None

    input_total, _ = lax.scan(hidden_step, jnp.zeros((tokens, D), jnp.float32), jnp.arange(N_COL, dtype=jnp.int32))
    input_grad = input_total.astype(jnp.bfloat16)
    contract = (((0,), (0,)), ((), ()))
    gate_wgrad = lax.dot_general(inputs, gate_delta, contract, preferred_element_type=jnp.float32).astype(jnp.bfloat16)
    up_wgrad = lax.dot_general(inputs, up_delta, contract, preferred_element_type=jnp.float32).astype(jnp.bfloat16)
    down_wgrad = lax.dot_general(hidden, out_grad, contract, preferred_element_type=jnp.float32).astype(jnp.bfloat16)
    return input_grad, gate_wgrad, up_wgrad, down_wgrad
```

```python
import functools

import jax
import jax.numpy as jnp
from jax import lax
from jax.experimental import pallas as pl
from jax.experimental.pallas import tpu as pltpu
from jax.sharding import PartitionSpec as P

MESH = pl.DeviceIdType.MESH
BF16, F32 = jnp.bfloat16, jnp.float32
REST = (((1,), (1,)), ((), ()))


def remote(src, dst, send, recv, device):
    return pltpu.make_async_remote_copy(
        src_ref=src, dst_ref=dst, send_sem=send, recv_sem=recv, device_id=device, device_id_type=MESH
    )


def kernel(
    nr, nc, fc,
    x_ref, g_ref, wg_ref, wu_ref, wd_ref,
    ig_ref, xo_ref, go_ref, ho_ref, gdo_ref, udo_ref,
    xg, wgu, wdv, part, inb, exb, res, acc, pair_out, pair_in, sum_out, chip_in,
    own_sem, w_sem, ag_send, ag_recv, fw_send, in_send, in_recv, ex_recv, res_send, res_recv,
    out_sem, act_sem, pair_send, pair_recv, chip_send, chip_recv,
):
    row, col = lax.axis_index("row"), lax.axis_index("col")
    tl, dl = x_ref.shape
    nch = wgu.shape[0]
    chips = nc // 2
    core, chip = lax.rem(col, 2), col // 2
    sibling = chip * 2 + 1 - core
    half = nr // 2
    low = row < half
    inward = jnp.where(low, row + 1, row - 1)
    outward = jnp.where(low, row - 1, row + 1)
    mid = jnp.logical_or(row == half - 1, row == half)
    edge = jnp.logical_or(row == 0, row == nr - 1)
    not_mid, not_edge = jnp.logical_not(mid), jnp.logical_not(edge)

    def peer(k):
        return lax.rem(chip + k, chips) * 2 + core

    def source(k):
        return lax.rem(chip + chips - k, chips) * 2 + core

    def tokens(b):
        return pl.ds(pl.multiple_of(b * tl, tl), tl)

    def hid(c):
        return pl.ds(pl.multiple_of(c * fc, fc), fc)

    def weights(c):
        return (
            pltpu.make_async_copy(wg_ref.at[:, hid(c)], wgu.at[c, :, pl.ds(0, fc)], w_sem.at[0, c]),
            pltpu.make_async_copy(wu_ref.at[:, hid(c)], wgu.at[c, :, pl.ds(fc, fc)], w_sem.at[1, c]),
            pltpu.make_async_copy(wd_ref.at[hid(c), :], wdv.at[c], w_sem.at[2, c]),
        )

    blocks = (x_ref, g_ref)

    def own(a):
        return pltpu.make_async_copy(blocks[a], xg.at[a, tokens(col), :], own_sem.at[a])

    for a in range(2):
        own(a).start()

    barrier = pltpu.get_barrier_semaphore()
    pl.semaphore_signal(barrier, inc=1, device_id=(row, sibling), device_id_type=MESH)
    for k in range(1, chips):
        pl.semaphore_signal(barrier, inc=1, device_id=(row, peer(k)), device_id_type=MESH)
    pl.semaphore_signal(barrier, inc=1, device_id=(inward, col), device_id_type=MESH)

    @pl.when(not_edge)
    def _():
        pl.semaphore_signal(barrier, inc=1, device_id=(outward, col), device_id_type=MESH)

    pl.semaphore_wait(barrier, chips + 1 + jnp.where(edge, 0, 1))

    def direct(a, k):
        to = peer(k) if k else sibling
        return remote(
            blocks[a], xg.at[a, tokens(col), :], ag_send.at[a, k], ag_recv.at[a, col], (row, to)
        )

    def forward(a, k):
        rows = tokens(source(k))
        return remote(
            xg.at[a, rows, :], xg.at[a, rows, :], fw_send.at[a, k], ag_recv.at[a, source(k)], (row, sibling)
        )

    def arrived(a, b):
        rows = tokens(b)
        return remote(xg.at[a, rows, :], xg.at[a, rows, :], fw_send.at[a, 0], ag_recv.at[a, b], (row, sibling))

    for a in range(2):
        for k in list(range(1, chips)) + [0]:
            direct(a, k).start()

    def load(c, _):
        for copy in weights(c):
            copy.start()
        return 0

    lax.fori_loop(0, nch, load, 0)
    acc[...] = jnp.zeros_like(acc)

    for a in range(2):
        own(a).wait()
        for k in range(1, chips):
            arrived(a, source(k)).wait_recv()
            forward(a, k).start()
    for a in range(2):
        arrived(a, sibling).wait_recv()
        for k in range(1, chips):
            arrived(a, source(k) + 1 - 2 * core).wait_recv()

    acts = (
        pltpu.make_async_copy(xg.at[0], xo_ref, act_sem.at[0]),
        pltpu.make_async_copy(xg.at[1], go_ref, act_sem.at[1]),
    )
    for copy in acts:
        copy.start()

    def inner(c):
        return remote(part.at[c], inb.at[c], in_send.at[c], in_recv.at[c], (inward, col))

    def exchange(c):
        return remote(part.at[c], exb.at[c], in_send.at[c], ex_recv.at[c], (inward, col))

    def result(c):
        return remote(res.at[c], res.at[c], res_send.at[c], res_recv.at[c], (outward, col))

    def outs(c):
        return (
            pltpu.make_async_copy(res.at[c, :, pl.ds(0, fc)], ho_ref.at[:, hid(c)], out_sem.at[0, c]),
            pltpu.make_async_copy(res.at[c, :, pl.ds(fc, fc)], gdo_ref.at[:, hid(c)], out_sem.at[1, c]),
            pltpu.make_async_copy(res.at[c, :, pl.ds(2 * fc, fc)], udo_ref.at[:, hid(c)], out_sem.at[2, c]),
        )

    def back(c):
        for copy in outs(c):
            copy.start()
        deltas = res[c, :, fc:]
        piece = min(512, dl)
        for p in range(dl // piece):
            cols = slice(p * piece, (p + 1) * piece)
            acc[:, cols] += lax.dot_general(deltas, wgu[c, cols, :], REST, preferred_element_type=F32)

    def step(c, _):
        @pl.when(c < nch)
        def _():
            for copy in weights(c):
                copy.wait()
            part[c, :, : 2 * fc] = jnp.dot(xg[0], wgu[c], preferred_element_type=F32).astype(BF16)
            part[c, :, 2 * fc :] = lax.dot_general(
                xg[1], wdv[c], REST, preferred_element_type=F32
            ).astype(BF16)

            @pl.when(not_edge)
            def _():
                inner(c).wait_recv()
                part[c] = (part[c].astype(F32) + inb[c].astype(F32)).astype(BF16)

            @pl.when(mid)
            def _():
                exchange(c).start()

            @pl.when(not_mid)
            def _():
                inner(c).start()

        @pl.when(jnp.logical_and(mid, c > 0))
        def _():
            b = c - 1
            exchange(b).wait_recv()

            def summed(i):
                cols = slice(i * fc, (i + 1) * fc)
                return part[b, :, cols].astype(F32) + exb[b, :, cols].astype(F32)

            gate, up, grad = summed(0), summed(1), summed(2)
            sig = jax.nn.sigmoid(gate)
            act = gate * sig
            res[b, :, :fc] = (act * up).astype(BF16)
            res[b, :, fc : 2 * fc] = (grad * up * sig * (1.0 + gate * (1.0 - sig))).astype(BF16)
            res[b, :, 2 * fc :] = (grad * act).astype(BF16)

            @pl.when(not_edge)
            def _():
                result(b).start()

            back(b)

        return 0

    lax.fori_loop(0, nch + 1, step, 0)

    @pl.when(not_mid)
    def _():
        def take(c, _):
            result(c).wait_recv()

            @pl.when(not_edge)
            def _():
                result(c).start()

            back(c)
            return 0

        lax.fori_loop(0, nch, take, 0)

    def pair(j):
        return remote(
            pair_out.at[j], pair_in.at[j], pair_send.at[j], pair_recv.at[j], (row, sibling)
        )

    def across(j, owner):
        return remote(
            sum_out.at[j], chip_in.at[chip], chip_send.at[j], chip_recv.at[chip], (row, owner)
        )

    order = [lax.rem(chip + k, chips) for k in list(range(1, chips)) + [0]]
    for j in order:
        pair_out[j] = acc[tokens(2 * j + 1 - core), :].astype(BF16)
        pair(j).start()
    for j in order[:-1]:
        pair(j).wait_recv()
        sum_out[j] = (acc[tokens(2 * j + core), :] + pair_in[j].astype(F32)).astype(BF16)
        across(j, 2 * j + core).start()
    pair(chip).wait_recv()
    total = acc[tokens(col), :] + pair_in[chip].astype(F32)
    for j in order[:-1]:
        remote(sum_out.at[j], chip_in.at[j], chip_send.at[j], chip_recv.at[j], (row, 2 * j + core)).wait_recv()
        total = total + chip_in[j].astype(F32)
    ig_ref[...] = total.astype(BF16)

    for a in range(2):
        for k in range(chips):
            direct(a, k).wait_send()
        for k in range(1, chips):
            forward(a, k).wait_send()
        acts[a].wait()

    def drain(c, _):
        inner(c).wait_send()

        @pl.when(not_edge)
        def _():
            result(c).wait_send()

        for copy in outs(c):
            copy.wait()
        return 0

    lax.fori_loop(0, nch, drain, 0)
    for j in order:
        pair(j).wait_send()
    for j in order[:-1]:
        across(j, 2 * j + core).wait_send()


def on_device(nr, nc, x, g, wg, wu, wd):
    tl, dl = x.shape
    fl = wg.shape[1]
    rows = tl * nc
    fc = min(128, fl)
    nch = fl // fc
    chips = nc // 2
    dma = pltpu.SemaphoreType.DMA
    any_spec = pl.BlockSpec(memory_space=pl.ANY)
    acts = jax.ShapeDtypeStruct((rows, dl), BF16)
    hids = jax.ShapeDtypeStruct((rows, fl), BF16)
    flops = 10 * rows * dl * fl
    grad, x_all, g_all, hidden, gate_delta, up_delta = pl.pallas_call(
        functools.partial(kernel, nr, nc, fc),
        out_shape=(jax.ShapeDtypeStruct((tl, dl), BF16), acts, acts, hids, hids, hids),
        in_specs=[any_spec] * 5,
        out_specs=(pl.BlockSpec(memory_space=pltpu.VMEM),) + (any_spec,) * 5,
        scratch_shapes=[
            pltpu.VMEM((2, rows, dl), BF16),
            pltpu.VMEM((nch, dl, 2 * fc), BF16),
            pltpu.VMEM((nch, fc, dl), BF16),
            pltpu.VMEM((nch, rows, 3 * fc), BF16),
            pltpu.VMEM((nch, rows, 3 * fc), BF16),
            pltpu.VMEM((nch, rows, 3 * fc), BF16),
            pltpu.VMEM((nch, rows, 3 * fc), BF16),
            pltpu.VMEM((rows, dl), F32),
            pltpu.VMEM((chips, tl, dl), BF16),
            pltpu.VMEM((chips, tl, dl), BF16),
            pltpu.VMEM((chips, tl, dl), BF16),
            pltpu.VMEM((chips, tl, dl), BF16),
            dma((2,)),
            dma((3, nch)),
            dma((2, chips)),
            dma((2, nc)),
            dma((2, chips)),
            dma((nch,)),
            dma((nch,)),
            dma((nch,)),
            dma((nch,)),
            dma((nch,)),
            dma((3, nch)),
            dma((2,)),
            dma((chips,)),
            dma((chips,)),
            dma((chips,)),
            dma((chips,)),
        ],
        compiler_params=pltpu.CompilerParams(
            collective_id=0, has_side_effects=True, vmem_limit_bytes=56 * 2**20
        ),
        cost_estimate=pl.CostEstimate(flops=flops, bytes_accessed=6 * dl * fl, transcendentals=rows * fl),
    )(x, g, wg, wu, wd)
    contract = (((0,), (0,)), ((), ()))

    def wgrad(a, b):
        return lax.dot_general(a, b, contract, preferred_element_type=F32).astype(BF16)

    return grad, wgrad(x_all, gate_delta), wgrad(x_all, up_delta), wgrad(hidden, g_all)


def solution(mesh):
    in_specs = (P("col", "row"), P("col", "row"), P("row", "col"), P("row", "col"), P("col", "row"))
    out_specs = (P("col", "row"), P("row", "col"), P("row", "col"), P("col", "row"))
    return jax.shard_map(
        functools.partial(on_device, mesh.shape["row"], mesh.shape["col"]),
        mesh=mesh, in_specs=in_specs, out_specs=out_specs, check_vma=False,
    )
```

```python
import functools

import jax
import jax.numpy as jnp
from jax import lax
from jax.experimental import pallas as pl
from jax.experimental.pallas import tpu as pltpu
from jax.sharding import PartitionSpec as P

MESH = pl.DeviceIdType.MESH
BF16, F32 = jnp.bfloat16, jnp.float32
REST = (((1,), (1,)), ((), ()))
LAG = 2


def remote(src, dst, send, recv, device):
    return pltpu.make_async_remote_copy(
        src_ref=src, dst_ref=dst, send_sem=send, recv_sem=recv, device_id=device, device_id_type=MESH
    )


def kernel(
    nr, nc, fc,
    x_ref, g_ref, wg_ref, wu_ref, wd_ref,
    ig_ref, xo_ref, go_ref, ho_ref, gdo_ref, udo_ref,
    xg, wgu, wdv, part, inb, exb, res, acc, pair_out, pair_in, sum_out, chip_in,
    own_sem, w_sem, ag_send, ag_recv, fw_send, in_send, in_recv, ex_recv, res_send, res_recv,
    out_sem, act_sem, pair_send, pair_recv, chip_send, chip_recv,
):
    row, col = lax.axis_index("row"), lax.axis_index("col")
    tl, dl = x_ref.shape
    nch = wgu.shape[0]
    chips = nc // 2
    tg = 2 * tl
    units = chips * nch
    core, chip = lax.rem(col, 2), col // 2
    sibling = chip * 2 + 1 - core
    half = nr // 2
    low = row < half
    inward = jnp.where(low, row + 1, row - 1)
    outward = jnp.where(low, row - 1, row + 1)
    mid = jnp.logical_or(row == half - 1, row == half)
    edge = jnp.logical_or(row == 0, row == nr - 1)
    not_mid, not_edge = jnp.logical_not(mid), jnp.logical_not(edge)
    mine = pl.ds(pl.multiple_of(core * tl, tl), tl)
    other = pl.ds(pl.multiple_of((1 - core) * tl, tl), tl)
    blocks = (x_ref, g_ref)

    def peer(k):
        return lax.rem(chip + k, chips) * 2 + core

    def owner(k):
        return lax.rem(chip + chips - k, chips) * 2 + core

    def hid(c):
        return pl.ds(pl.multiple_of(c * fc, fc), fc)

    def weights(c):
        return (
            pltpu.make_async_copy(wg_ref.at[:, hid(c)], wgu.at[c, :, pl.ds(0, fc)], w_sem.at[0, c]),
            pltpu.make_async_copy(wu_ref.at[:, hid(c)], wgu.at[c, :, pl.ds(fc, fc)], w_sem.at[1, c]),
            pltpu.make_async_copy(wd_ref.at[hid(c), :], wdv.at[c], w_sem.at[2, c]),
        )

    def own(a):
        return pltpu.make_async_copy(blocks[a], xg.at[a, 0, mine, :], own_sem.at[a])

    for a in range(2):
        own(a).start()

    barrier = pltpu.get_barrier_semaphore()
    pl.semaphore_signal(barrier, inc=1, device_id=(row, sibling), device_id_type=MESH)
    for k in range(1, chips):
        pl.semaphore_signal(barrier, inc=1, device_id=(row, peer(k)), device_id_type=MESH)
    pl.semaphore_signal(barrier, inc=1, device_id=(inward, col), device_id_type=MESH)

    @pl.when(not_edge)
    def _():
        pl.semaphore_signal(barrier, inc=1, device_id=(outward, col), device_id_type=MESH)

    for copy in weights(0):
        copy.start()
    pl.semaphore_wait(barrier, chips + 1 + jnp.where(edge, 0, 1))

    def direct(a, k):
        return remote(
            blocks[a], xg.at[a, k, mine, :], ag_send.at[a, k], ag_recv.at[a, k, 0],
            (row, peer(k) if k else sibling),
        )

    def came(a, k):
        return remote(
            xg.at[a, k, mine, :], xg.at[a, k, mine, :], fw_send.at[a, k], ag_recv.at[a, k, 0], (row, sibling)
        )

    def forward(a, k):
        return remote(
            xg.at[a, k, mine, :], xg.at[a, k, mine, :], fw_send.at[a, k], ag_recv.at[a, k, 1], (row, sibling)
        )

    def forwarded(a, k):
        return remote(
            xg.at[a, k, other, :], xg.at[a, k, other, :], fw_send.at[a, k], ag_recv.at[a, k, 1], (row, sibling)
        )

    for k in range(chips):
        for a in range(2):
            direct(a, k).start()

    def load(c, _):
        for copy in weights(c):
            copy.start()
        return 0

    lax.fori_loop(1, nch, load, 0)
    acc[...] = jnp.zeros_like(acc)

    for a in range(2):
        own(a).wait()
        remote(
            xg.at[a, 0, other, :], xg.at[a, 0, other, :], fw_send.at[a, 0], ag_recv.at[a, 0, 0], (row, sibling)
        ).wait_recv()

    def inner(u):
        return remote(part.at[u], inb.at[u], in_send.at[u], in_recv.at[u], (inward, col))

    def exchange(u):
        return remote(part.at[u], exb.at[u], in_send.at[u], ex_recv.at[u], (inward, col))

    def result(u):
        return remote(res.at[u], res.at[u], res_send.at[u], res_recv.at[u], (outward, col))

    def outs(u):
        k, c = u // nch, lax.rem(u, nch)
        rows = pl.ds(pl.multiple_of(k * tg, tg), tg)
        return [
            pltpu.make_async_copy(
                res.at[u, :, pl.ds(i * fc, fc)], ref.at[rows, hid(c)], out_sem.at[i, u]
            )
            for i, ref in enumerate((ho_ref, gdo_ref, udo_ref))
        ]

    def pair(k):
        return remote(
            pair_out.at[k], pair_in.at[k], pair_send.at[k], pair_recv.at[k], (row, sibling)
        )

    def across(k):
        return remote(
            sum_out.at[k], chip_in.at[k], chip_send.at[k], chip_recv.at[k], (row, owner(k))
        )

    def settle(k):
        pair(k).wait_recv()
        sum_out[k] = (acc[k, mine, :] + pair_in[k].astype(F32)).astype(BF16)
        across(k).start()

    def back(u):
        k, c = u // nch, lax.rem(u, nch)
        for copy in outs(u):
            copy.start()
        deltas = res[u, :, fc:]
        piece = min(512, dl)
        for p in range(dl // piece):
            cols = slice(p * piece, (p + 1) * piece)
            acc[k, :, cols] += lax.dot_general(deltas, wgu[c, cols, :], REST, preferred_element_type=F32)

        @pl.when(jnp.logical_and(c == nch // 2, k > 1))
        def _():
            settle(k - 1)

        @pl.when(c == nch - 1)
        def _():
            pair_out[k] = acc[k, other, :].astype(BF16)
            pair(k).start()

    def step(u, _):
        @pl.when(u < units)
        def _():
            k, c = u // nch, lax.rem(u, nch)

            @pl.when(k == 0)
            def _():
                for copy in weights(c):
                    copy.wait()

            @pl.when(jnp.logical_and(k > 0, c == 0))
            def _():
                for a in range(2):
                    forwarded(a, k).wait_recv()

            part[u, :, : 2 * fc] = jnp.dot(xg[0, k], wgu[c], preferred_element_type=F32).astype(BF16)
            part[u, :, 2 * fc :] = lax.dot_general(
                xg[1, k], wdv[c], REST, preferred_element_type=F32
            ).astype(BF16)

            @pl.when(not_edge)
            def _():
                inner(u).wait_recv()
                part[u] = (part[u].astype(F32) + inb[u].astype(F32)).astype(BF16)

            @pl.when(mid)
            def _():
                exchange(u).start()

            @pl.when(not_mid)
            def _():
                inner(u).start()

            @pl.when(jnp.logical_and(c == nch // 2, k + 1 < chips))
            def _():
                for a in range(2):
                    came(a, k + 1).wait_recv()
                    forward(a, k + 1).start()

        @pl.when(jnp.logical_and(mid, u >= LAG))
        def _():
            v = u - LAG
            exchange(v).wait_recv()

            def summed(i):
                cols = slice(i * fc, (i + 1) * fc)
                return part[v, :, cols].astype(F32) + exb[v, :, cols].astype(F32)

            gate, up, grad = summed(0), summed(1), summed(2)
            sig = jax.nn.sigmoid(gate)
            act = gate * sig
            res[v, :, :fc] = (act * up).astype(BF16)
            res[v, :, fc : 2 * fc] = (grad * up * sig * (1.0 + gate * (1.0 - sig))).astype(BF16)
            res[v, :, 2 * fc :] = (grad * act).astype(BF16)

            @pl.when(not_edge)
            def _():
                result(v).start()

            back(v)

        return 0

    lax.fori_loop(0, units + LAG, step, 0)

    acts = (
        pltpu.make_async_copy(xg.at[0], xo_ref, act_sem.at[0]),
        pltpu.make_async_copy(xg.at[1], go_ref, act_sem.at[1]),
    )
    for copy in acts:
        copy.start()

    @pl.when(not_mid)
    def _():
        def take(u, _):
            result(u).wait_recv()

            @pl.when(not_edge)
            def _():
                result(u).start()

            back(u)
            return 0

        lax.fori_loop(0, units, take, 0)

    if chips > 1:
        settle(chips - 1)
    pair(0).wait_recv()
    total = acc[0, mine, :] + pair_in[0].astype(F32)
    for k in range(1, chips):
        across(k).wait_recv()
        total = total + chip_in[k].astype(F32)
    ig_ref[...] = total.astype(BF16)

    for a in range(2):
        for k in range(chips):
            direct(a, k).wait_send()
        for k in range(1, chips):
            forward(a, k).wait_send()
        acts[a].wait()

    def drain(u, _):
        inner(u).wait_send()

        @pl.when(not_edge)
        def _():
            result(u).wait_send()

        for copy in outs(u):
            copy.wait()
        return 0

    lax.fori_loop(0, units, drain, 0)
    for k in range(chips):
        pair(k).wait_send()
    for k in range(1, chips):
        across(k).wait_send()


def on_device(nr, nc, x, g, wg, wu, wd):
    tl, dl = x.shape
    fl = wg.shape[1]
    rows = tl * nc
    fc = min(256, fl)
    nch = fl // fc
    chips = nc // 2
    tg = 2 * tl
    units = chips * nch
    dma = pltpu.SemaphoreType.DMA
    any_spec = pl.BlockSpec(memory_space=pl.ANY)
    acts = jax.ShapeDtypeStruct((chips, tg, dl), BF16)
    hids = jax.ShapeDtypeStruct((rows, fl), BF16)
    flops = 10 * rows * dl * fl
    grad, x_all, g_all, hidden, gate_delta, up_delta = pl.pallas_call(
        functools.partial(kernel, nr, nc, fc),
        out_shape=(jax.ShapeDtypeStruct((tl, dl), BF16), acts, acts, hids, hids, hids),
        in_specs=[any_spec] * 5,
        out_specs=(pl.BlockSpec(memory_space=pltpu.VMEM),) + (any_spec,) * 5,
        scratch_shapes=[
            pltpu.VMEM((2, chips, tg, dl), BF16),
            pltpu.VMEM((nch, dl, 2 * fc), BF16),
            pltpu.VMEM((nch, fc, dl), BF16),
            pltpu.VMEM((units, tg, 3 * fc), BF16),
            pltpu.VMEM((units, tg, 3 * fc), BF16),
            pltpu.VMEM((units, tg, 3 * fc), BF16),
            pltpu.VMEM((units, tg, 3 * fc), BF16),
            pltpu.VMEM((chips, tg, dl), F32),
            pltpu.VMEM((chips, tl, dl), BF16),
            pltpu.VMEM((chips, tl, dl), BF16),
            pltpu.VMEM((chips, tl, dl), BF16),
            pltpu.VMEM((chips, tl, dl), BF16),
            dma((2,)),
            dma((3, nch)),
            dma((2, chips)),
            dma((2, chips, 2)),
            dma((2, chips)),
            dma((units,)),
            dma((units,)),
            dma((units,)),
            dma((units,)),
            dma((units,)),
            dma((3, units)),
            dma((2,)),
            dma((chips,)),
            dma((chips,)),
            dma((chips,)),
            dma((chips,)),
        ],
        compiler_params=pltpu.CompilerParams(
            collective_id=0, has_side_effects=True, vmem_limit_bytes=56 * 2**20
        ),
        cost_estimate=pl.CostEstimate(flops=flops, bytes_accessed=6 * dl * fl, transcendentals=rows * fl),
    )(x, g, wg, wu, wd)
    x_all, g_all = x_all.reshape(rows, dl), g_all.reshape(rows, dl)
    contract = (((0,), (0,)), ((), ()))

    def wgrad(a, b):
        return lax.dot_general(a, b, contract, preferred_element_type=F32).astype(BF16)

    return grad, wgrad(x_all, gate_delta), wgrad(x_all, up_delta), wgrad(hidden, g_all)


def solution(mesh):
    in_specs = (P("col", "row"), P("col", "row"), P("row", "col"), P("row", "col"), P("col", "row"))
    out_specs = (P("col", "row"), P("row", "col"), P("row", "col"), P("col", "row"))
    return jax.shard_map(
        functools.partial(on_device, mesh.shape["row"], mesh.shape["col"]),
        mesh=mesh, in_specs=in_specs, out_specs=out_specs, check_vma=False,
    )
```

```python
import functools

import jax
import jax.numpy as jnp
from jax import lax
from jax.experimental import pallas as pl
from jax.experimental.pallas import tpu as pltpu
from jax.sharding import PartitionSpec as P

MESH = pl.DeviceIdType.MESH
BF16, F32 = jnp.bfloat16, jnp.float32
REST = (((1,), (1,)), ((), ()))
LAG = 2
TILE = 256


def remote(src, dst, send, recv, device):
    return pltpu.make_async_remote_copy(
        src_ref=src, dst_ref=dst, send_sem=send, recv_sem=recv, device_id=device, device_id_type=MESH
    )


def kernel(
    nr, nc, fc,
    x_ref, g_ref, wg_ref, wu_ref, wd_ref,
    ig_ref, xo_ref, go_ref, ho_ref, gdo_ref, udo_ref,
    xg, wgu, wdv, part, inb, exb, res, acc, pair_out, pair_in, sum_out, chip_in,
    own_sem, w_sem, ag_send, ag_recv, fw_send, in_send, in_recv, ex_recv, res_send, res_recv,
    out_sem, act_sem, pair_send, pair_recv, chip_send, chip_recv,
):
    row, col = lax.axis_index("row"), lax.axis_index("col")
    tl, dl = x_ref.shape
    nch = wgu.shape[0]
    chips = nc // 2
    tg = 2 * tl
    units = chips * nch
    core, chip = lax.rem(col, 2), col // 2
    sibling = chip * 2 + 1 - core
    half = nr // 2
    low = row < half
    inward = jnp.where(low, row + 1, row - 1)
    outward = jnp.where(low, row - 1, row + 1)
    mid = jnp.logical_or(row == half - 1, row == half)
    edge = jnp.logical_or(row == 0, row == nr - 1)
    not_mid, not_edge = jnp.logical_not(mid), jnp.logical_not(edge)
    mine = pl.ds(pl.multiple_of(core * tl, tl), tl)
    other = pl.ds(pl.multiple_of((1 - core) * tl, tl), tl)
    blocks = (x_ref, g_ref)

    def peer(k):
        return lax.rem(chip + k, chips) * 2 + core

    def owner(k):
        return lax.rem(chip + chips - k, chips) * 2 + core

    def hid(c):
        return pl.ds(pl.multiple_of(c * fc, fc), fc)

    def weights(c):
        return (
            pltpu.make_async_copy(wg_ref.at[:, hid(c)], wgu.at[c, :, pl.ds(0, fc)], w_sem.at[0, c]),
            pltpu.make_async_copy(wu_ref.at[:, hid(c)], wgu.at[c, :, pl.ds(fc, fc)], w_sem.at[1, c]),
            pltpu.make_async_copy(wd_ref.at[hid(c), :], wdv.at[c], w_sem.at[2, c]),
        )

    def own(a):
        return pltpu.make_async_copy(blocks[a], xg.at[a, 0, mine, :], own_sem.at[a])

    for a in range(2):
        own(a).start()

    barrier = pltpu.get_barrier_semaphore()
    pl.semaphore_signal(barrier, inc=1, device_id=(row, sibling), device_id_type=MESH)
    for k in range(1, chips):
        pl.semaphore_signal(barrier, inc=1, device_id=(row, peer(k)), device_id_type=MESH)
    pl.semaphore_signal(barrier, inc=1, device_id=(inward, col), device_id_type=MESH)

    @pl.when(not_edge)
    def _():
        pl.semaphore_signal(barrier, inc=1, device_id=(outward, col), device_id_type=MESH)

    for copy in weights(0):
        copy.start()
    pl.semaphore_wait(barrier, chips + 1 + jnp.where(edge, 0, 1))

    def direct(a, k):
        return remote(
            blocks[a], xg.at[a, k, mine, :], ag_send.at[a, k], ag_recv.at[a, k, 0],
            (row, peer(k) if k else sibling),
        )

    def came(a, k):
        return remote(
            xg.at[a, k, mine, :], xg.at[a, k, mine, :], fw_send.at[a, k], ag_recv.at[a, k, 0], (row, sibling)
        )

    def forward(a, k):
        return remote(
            xg.at[a, k, mine, :], xg.at[a, k, mine, :], fw_send.at[a, k], ag_recv.at[a, k, 1], (row, sibling)
        )

    def forwarded(a, k):
        return remote(
            xg.at[a, k, other, :], xg.at[a, k, other, :], fw_send.at[a, k], ag_recv.at[a, k, 1], (row, sibling)
        )

    for k in range(chips):
        for a in range(2):
            direct(a, k).start()

    def load(c, _):
        for copy in weights(c):
            copy.start()
        return 0

    lax.fori_loop(1, nch, load, 0)
    acc[...] = jnp.zeros_like(acc)

    for a in range(2):
        own(a).wait()
        remote(
            xg.at[a, 0, other, :], xg.at[a, 0, other, :], fw_send.at[a, 0], ag_recv.at[a, 0, 0], (row, sibling)
        ).wait_recv()

    def inner(u):
        return remote(part.at[u], inb.at[u], in_send.at[u], in_recv.at[u], (inward, col))

    def exchange(u):
        return remote(part.at[u], exb.at[u], in_send.at[u], ex_recv.at[u], (inward, col))

    def result(u):
        return remote(res.at[u], res.at[u], res_send.at[u], res_recv.at[u], (outward, col))

    def outs(u):
        k, c = u // nch, lax.rem(u, nch)
        rows = pl.ds(pl.multiple_of(k * tg, tg), tg)
        return [
            pltpu.make_async_copy(
                res.at[u, :, pl.ds(i * fc, fc)], ref.at[rows, hid(c)], out_sem.at[i, u]
            )
            for i, ref in enumerate((ho_ref, gdo_ref, udo_ref))
        ]

    def pair(k):
        return remote(
            pair_out.at[k], pair_in.at[k], pair_send.at[k], pair_recv.at[k], (row, sibling)
        )

    def across(k):
        return remote(
            sum_out.at[k], chip_in.at[k], chip_send.at[k], chip_recv.at[k], (row, owner(k))
        )

    def settle(k):
        pair(k).wait_recv()
        sum_out[k] = (acc[k, mine, :] + pair_in[k].astype(F32)).astype(BF16)
        across(k).start()

    def back(u):
        k, c = u // nch, lax.rem(u, nch)
        for copy in outs(u):
            copy.start()
        deltas = res[u, :, fc:]
        piece = min(512, dl)
        for p in range(dl // piece):
            cols = slice(p * piece, (p + 1) * piece)
            acc[k, :, cols] += lax.dot_general(deltas, wgu[c, cols, :], REST, preferred_element_type=F32)

        @pl.when(jnp.logical_and(c == nch // 2, k > 1))
        def _():
            settle(k - 1)

        @pl.when(c == nch - 1)
        def _():
            pair_out[k] = acc[k, other, :].astype(BF16)
            pair(k).start()

    def step(u, _):
        @pl.when(u < units)
        def _():
            k, c = u // nch, lax.rem(u, nch)

            @pl.when(k == 0)
            def _():
                for copy in weights(c):
                    copy.wait()

            @pl.when(jnp.logical_and(k > 0, c == 0))
            def _():
                for a in range(2):
                    forwarded(a, k).wait_recv()

            part[u, :, : 2 * fc] = jnp.dot(xg[0, k], wgu[c], preferred_element_type=F32).astype(BF16)
            part[u, :, 2 * fc :] = lax.dot_general(
                xg[1, k], wdv[c], REST, preferred_element_type=F32
            ).astype(BF16)

            @pl.when(not_edge)
            def _():
                inner(u).wait_recv()
                part[u] = (part[u].astype(F32) + inb[u].astype(F32)).astype(BF16)

            @pl.when(mid)
            def _():
                exchange(u).start()

            @pl.when(not_mid)
            def _():
                inner(u).start()

            @pl.when(jnp.logical_and(c == nch // 2, k + 1 < chips))
            def _():
                for a in range(2):
                    came(a, k + 1).wait_recv()
                    forward(a, k + 1).start()

        @pl.when(jnp.logical_and(mid, u >= LAG))
        def _():
            v = u - LAG
            exchange(v).wait_recv()

            def summed(i):
                cols = slice(i * fc, (i + 1) * fc)
                return part[v, :, cols].astype(F32) + exb[v, :, cols].astype(F32)

            gate, up, grad = summed(0), summed(1), summed(2)
            sig = jax.nn.sigmoid(gate)
            act = gate * sig
            res[v, :, :fc] = (act * up).astype(BF16)
            res[v, :, fc : 2 * fc] = (grad * up * sig * (1.0 + gate * (1.0 - sig))).astype(BF16)
            res[v, :, 2 * fc :] = (grad * act).astype(BF16)

            @pl.when(not_edge)
            def _():
                result(v).start()

            back(v)

        return 0

    lax.fori_loop(0, units + LAG, step, 0)

    acts = (
        pltpu.make_async_copy(xg.at[0], xo_ref, act_sem.at[0]),
        pltpu.make_async_copy(xg.at[1], go_ref, act_sem.at[1]),
    )
    for copy in acts:
        copy.start()

    @pl.when(not_mid)
    def _():
        def take(u, _):
            result(u).wait_recv()

            @pl.when(not_edge)
            def _():
                result(u).start()

            back(u)
            return 0

        lax.fori_loop(0, units, take, 0)

    if chips > 1:
        settle(chips - 1)
    pair(0).wait_recv()
    total = acc[0, mine, :] + pair_in[0].astype(F32)
    for k in range(1, chips):
        across(k).wait_recv()
        total = total + chip_in[k].astype(F32)
    ig_ref[...] = total.astype(BF16)

    for a in range(2):
        for k in range(chips):
            direct(a, k).wait_send()
        for k in range(1, chips):
            forward(a, k).wait_send()
        acts[a].wait()

    def drain(u, _):
        inner(u).wait_send()

        @pl.when(not_edge)
        def _():
            result(u).wait_send()

        for copy in outs(u):
            copy.wait()
        return 0

    lax.fori_loop(0, units, drain, 0)
    for k in range(chips):
        pair(k).wait_send()
    for k in range(1, chips):
        across(k).wait_send()


def products(x_ref, h_ref, g_ref, gd_ref, ud_ref, wg_ref, wu_ref, wd_ref):
    contract = (((0,), (0,)), ((), ()))
    for left, right, out in ((x_ref, gd_ref, wg_ref), (x_ref, ud_ref, wu_ref), (h_ref, g_ref, wd_ref)):
        width = out.shape[1]
        piece = min(512, width)
        for p in range(width // piece):
            cols = slice(p * piece, (p + 1) * piece)
            out[:, cols] = lax.dot_general(
                left[...], right[:, cols], contract, preferred_element_type=F32
            ).astype(BF16)


def weight_grads(x_all, g_all, hidden, gate_delta, up_delta):
    rows, dl = x_all.shape
    fl = hidden.shape[1]
    tiles = max(1, min(dl, fl) // TILE)
    dt, ft = dl // tiles, fl // tiles
    whole = lambda i: (0, 0)
    column = lambda i: (0, i)
    band = lambda i: (i, 0)
    return pl.pallas_call(
        products,
        grid=(tiles,),
        out_shape=(
            jax.ShapeDtypeStruct((dl, fl), BF16),
            jax.ShapeDtypeStruct((dl, fl), BF16),
            jax.ShapeDtypeStruct((fl, dl), BF16),
        ),
        in_specs=[
            pl.BlockSpec((rows, dt), column),
            pl.BlockSpec((rows, ft), column),
            pl.BlockSpec((rows, dl), whole),
            pl.BlockSpec((rows, fl), whole),
            pl.BlockSpec((rows, fl), whole),
        ],
        out_specs=(
            pl.BlockSpec((dt, fl), band),
            pl.BlockSpec((dt, fl), band),
            pl.BlockSpec((ft, dl), band),
        ),
        compiler_params=pltpu.CompilerParams(vmem_limit_bytes=60 * 2**20),
        cost_estimate=pl.CostEstimate(
            flops=6 * rows * dl * fl, bytes_accessed=6 * dl * fl + 10 * rows * dl, transcendentals=0
        ),
    )(x_all, hidden, g_all, gate_delta, up_delta)


def on_device(nr, nc, x, g, wg, wu, wd):
    tl, dl = x.shape
    fl = wg.shape[1]
    rows = tl * nc
    fc = min(256, fl)
    nch = fl // fc
    chips = nc // 2
    tg = 2 * tl
    units = chips * nch
    dma = pltpu.SemaphoreType.DMA
    any_spec = pl.BlockSpec(memory_space=pl.ANY)
    acts = jax.ShapeDtypeStruct((chips, tg, dl), BF16)
    hids = jax.ShapeDtypeStruct((rows, fl), BF16)
    flops = 10 * rows * dl * fl
    grad, x_all, g_all, hidden, gate_delta, up_delta = pl.pallas_call(
        functools.partial(kernel, nr, nc, fc),
        out_shape=(jax.ShapeDtypeStruct((tl, dl), BF16), acts, acts, hids, hids, hids),
        in_specs=[any_spec] * 5,
        out_specs=(pl.BlockSpec(memory_space=pltpu.VMEM),) + (any_spec,) * 5,
        scratch_shapes=[
            pltpu.VMEM((2, chips, tg, dl), BF16),
            pltpu.VMEM((nch, dl, 2 * fc), BF16),
            pltpu.VMEM((nch, fc, dl), BF16),
            pltpu.VMEM((units, tg, 3 * fc), BF16),
            pltpu.VMEM((units, tg, 3 * fc), BF16),
            pltpu.VMEM((units, tg, 3 * fc), BF16),
            pltpu.VMEM((units, tg, 3 * fc), BF16),
            pltpu.VMEM((chips, tg, dl), F32),
            pltpu.VMEM((chips, tl, dl), BF16),
            pltpu.VMEM((chips, tl, dl), BF16),
            pltpu.VMEM((chips, tl, dl), BF16),
            pltpu.VMEM((chips, tl, dl), BF16),
            dma((2,)),
            dma((3, nch)),
            dma((2, chips)),
            dma((2, chips, 2)),
            dma((2, chips)),
            dma((units,)),
            dma((units,)),
            dma((units,)),
            dma((units,)),
            dma((units,)),
            dma((3, units)),
            dma((2,)),
            dma((chips,)),
            dma((chips,)),
            dma((chips,)),
            dma((chips,)),
        ],
        compiler_params=pltpu.CompilerParams(
            collective_id=0, has_side_effects=True, vmem_limit_bytes=56 * 2**20
        ),
        cost_estimate=pl.CostEstimate(flops=flops, bytes_accessed=6 * dl * fl, transcendentals=rows * fl),
    )(x, g, wg, wu, wd)
    x_all, g_all = x_all.reshape(rows, dl), g_all.reshape(rows, dl)
    return (grad, *weight_grads(x_all, g_all, hidden, gate_delta, up_delta))


def solution(mesh):
    in_specs = (P("col", "row"), P("col", "row"), P("row", "col"), P("row", "col"), P("col", "row"))
    out_specs = (P("col", "row"), P("row", "col"), P("row", "col"), P("col", "row"))
    return jax.shard_map(
        functools.partial(on_device, mesh.shape["row"], mesh.shape["col"]),
        mesh=mesh, in_specs=in_specs, out_specs=out_specs, check_vma=False,
    )
```
